128 devices in a mesh: grp: 2 (over y_hi), dev: 64 (over z, x, y_lo, core).
Axes of the slice: x: 4, y: 4 (y_hi: 2, y_lo: 2; y = y_hi * 2 + y_lo), z: 4, core: 2. Of those that a mesh axis runs over, the one named last changes fastest.
Arguments:
- positions: float32 [3, 393216], P(None, ('grp', 'dev')), may hold values from -1 to 1
- strengths: float32 [3, 393216], P(None, ('grp', 'dev')), may hold values from -0.75 to 0.75
- plan: int32 [8, 128], P(None, ('grp', 'dev')), may hold values from 0 to 127, as said below
Outputs:
- velocity: float32 [3, 393216], P(None, ('grp', 'dev'))
- new_strengths: float32 [3, 393216], P(None, ('grp', 'dev'))
The draws below stay inside these ranges and needn't reach their ends.
Inputs may be any that keep to these rules, and one draw needn't show every extreme that they name: In round r every block b is paired with plan[r, b] = b XOR m_r, where m_r is the same for all blocks and has exactly two set bits, and the m_r of the 8 rounds are distinct; so each round pairs the blocks two by two and no two blocks meet twice.
All inputs are finite; a program needn't handle non-finite values.
Results may differ from the reference program's by a relative error of at most 0.0003.
Values sent between devices are 32-bit elements; how exact they have to be, the bound alone decides.
No kernel may reach another device: no remote copies, remote signals or barrier semaphores. Data moves between devices by JAX's collectives and lax.ppermute only.
A program may use at most 64 MiB of HBM per device.

```python
import math
import jax
import jax.numpy as jnp
import numpy as np
from jax import lax

PART_DEV = 3072
ROUNDS = 8
PARTICLES = 393216


def draw_strengths(key, part):
    key = jax.random.fold_in(key, 7)
    rising = 0.5 + 1.5 * jnp.arange(PARTICLES, dtype=jnp.float32) / PARTICLES
    values = jnp.clip(jax.random.normal(key, (3, PARTICLES), jnp.float32), -6.0, 6.0)
    return (0.05 * rising[None, :] * values).astype(jnp.float32)


def draw_plan(key, part):
    key = jax.random.fold_in(key, 11)
    blocks = PARTICLES // PART_DEV
    levels = blocks.bit_length() - 1
    pair_masks = np.array([1 << first | 1 << second for first in range(levels) for second in range(first + 1, levels)], dtype=np.int32)
    table = jnp.asarray(pair_masks, dtype=jnp.int32)
    picks = jax.random.permutation(key, pair_masks.shape[0])[:ROUNDS]
    offset_masks = table[picks]
    device_ids = jnp.arange(blocks, dtype=jnp.int32)
    return jnp.bitwise_xor(offset_masks[:, None].astype(jnp.int32), device_ids[None, :]).astype(jnp.int32)


def block_levels(rng, shape, pieces, smallest, top_value):
    level, own = 1.0, jax.random.fold_in(rng, 6)
    for dim, parts in pieces:
        heights = jnp.exp(jax.random.uniform(jax.random.fold_in(own, dim), (parts,), jnp.float32, smallest / len(pieces), top_value / len(pieces)))
        level = level * jnp.repeat(heights, shape[dim] // parts).reshape([-1 if axis == dim else 1 for axis in range(len(shape))])
    return level


def setup_inputs(seed: int = 0) -> dict:
    streams_of = jax.random.split(jax.random.key(seed), 4)
    positions = jnp.clip(jax.random.uniform(streams_of[0], (3, PARTICLES), jnp.float32, -1.0, 1.0) * block_levels(streams_of[0], (3, PARTICLES), ((1, 128),), -0.4, 0.0), -1.0, 1.0)
    strengths = draw_strengths(jax.random.fold_in(streams_of[3], 71), 0)
    plan = draw_plan(jax.random.fold_in(streams_of[3], 71), 0)
    return dict(positions=positions, strengths=strengths, plan=plan)


SMOOTH_SQ = 0.01
INV_FOUR_PI = 1.0 / (4.0 * math.pi)
STEP_RATE = 0.25

def cross_lists(first, second):
    return [first[1] * second[2] - first[2] * second[1], first[2] * second[0] - first[0] * second[2], first[0] * second[1] - first[1] * second[0]]

def induced(targets, sources):
    offsets = [targets[component][:, None] - sources[component][None, :] for component in range(3)]
    dist_sq = offsets[0] * offsets[0] + offsets[1] * offsets[1] + offsets[2] * offsets[2] + SMOOTH_SQ
    inverse = lax.rsqrt(dist_sq)
    cube = inverse * inverse * inverse
    fifth = 3.0 * cube * inverse * inverse
    source_str = [sources[3 + component][None, :] for component in range(3)]
    target_str = [targets[3 + component][:, None] for component in range(3)]
    swirl = cross_lists(offsets, source_str)
    spin = cross_lists(target_str, source_str)
    along = target_str[0] * offsets[0] + target_str[1] * offsets[1] + target_str[2] * offsets[2]
    rows = [lax.optimization_barrier(jnp.sum(cube * swirl[component], 1)) for component in range(3)]
    rows = rows + [lax.optimization_barrier(jnp.sum(cube * spin[component] - fifth * along * swirl[component], 1)) for component in range(3)]
    return -INV_FOUR_PI * jnp.stack(rows)

def reference(positions, strengths, plan):
    particles = jnp.concatenate([positions, strengths], 0)
    blocks = PARTICLES // PART_DEV

    def device_terms(index):
        targets = lax.dynamic_slice_in_dim(particles, (index * PART_DEV).astype(jnp.int32), PART_DEV, 1)
        source_ids = jnp.concatenate([index[None], plan[:, index]]).astype(jnp.int32)

        def add_block(total, source_id):
            sources = lax.dynamic_slice_in_dim(particles, (source_id * PART_DEV).astype(jnp.int32), PART_DEV, 1)
            return (total + induced(targets, sources), None)
        total, unused = lax.scan(add_block, jnp.zeros((6, PART_DEV), jnp.float32), source_ids)
        return total
    totals = lax.map(device_terms, jnp.arange(blocks, dtype=jnp.int32))
    totals = totals.transpose(1, 0, 2).reshape(6, PARTICLES)
    velocity = totals[:3]
    stretch = totals[3:]
    peak = jnp.sqrt(jnp.max(lax.optimization_barrier(jnp.sum(stretch * stretch, 0))))
    new_strengths = strengths + STEP_RATE / (peak + 1e-06) * stretch
    return (velocity, new_strengths)
```

```python
import functools
import math

import jax
import jax.numpy as jnp
from jax import lax
from jax.experimental import pallas as pl
from jax.experimental.pallas import tpu as pltpu
from jax.sharding import PartitionSpec as P

SMOOTH_SQ = 0.01
INV_FOUR_PI = 1.0 / (4.0 * math.pi)
STEP_RATE = 0.25
AXES = ("grp", "dev")
TILE = 1024
CHUNK = 512
PIECE = 64
LANES = 256
K_DIST = 48
ROWS3 = 32
ROWS5 = 80
BF16 = jnp.bfloat16
F32 = jnp.float32


def dot(left, right):
    return jnp.dot(left, right, preferred_element_type=F32)


def pieces(value, dtype, count):
    out = []
    for _ in range(count):
        head = value.astype(dtype).astype(F32)
        out.append(head)
        value = value - head
    return out


def cross_rows(first, second):
    return [
        first[1] * second[2] - first[2] * second[1],
        first[2] * second[0] - first[0] * second[2],
        first[0] * second[1] - first[1] * second[0],
    ]


def rows_of(block):
    return [block[k : k + 1, :] for k in range(block.shape[0])]


def pair_kernel(
    slots, pick_ref, src_ref, home_ref, carry_ref, out_ref, peak_ref,
    feat3, feat5, dist8, fs, ft, x3, x5, o3, o5, *bufs
):
    count = home_ref.shape[1]
    chunks = slots * count // CHUNK
    tiles = count // TILE
    first, second = bufs[:4], bufs[4:]

    largest = jnp.max(jnp.abs(src_ref[pick_ref[0], 3:6, :]))
    for slot in range(1, slots):
        largest = jnp.maximum(largest, jnp.max(jnp.abs(src_ref[pick_ref[slot], 3:6, :])))
    scale = jnp.maximum(largest, 1e-30)

    feat3[...] = jnp.zeros_like(feat3)
    dist8[...] = jnp.zeros_like(dist8)

    def fill(slot, _):
        block = src_ref[pick_ref[slot]]
        cols = pl.ds(pl.multiple_of(slot * count, count), count)
        pos = rows_of(block[0:3])
        strength = rows_of(block[3:6] / scale)
        moment = cross_rows(pos, strength)
        for k in range(3):
            feat3[k : k + 1, :] = strength[k]
            feat3[3 + k : 4 + k, :] = moment[k]
            feat5[k : k + 1, :] = strength[k]
            feat5[3 + k : 4 + k, :] = moment[k]
            for l in range(3):
                feat5[6 + 3 * k + l : 7 + 3 * k + l, :] = pos[k] * strength[l]
                feat5[15 + 3 * k + l : 16 + 3 * k + l, :] = pos[k] * moment[l]
            dist8[k : k + 1, :] = pos[k]
        dist8[3:4, :] = pos[0] * pos[0] + pos[1] * pos[1] + pos[2] * pos[2]
        dist8[4:5, :] = jnp.ones_like(pos[0])
        q = pieces(dist8[...], BF16, 3)
        rows = jnp.concatenate([q[0], q[0], q[1], q[1], q[0], q[2]], 0)
        rows = jnp.concatenate([rows, jnp.zeros((128 - K_DIST, count), F32)], 0)
        fs[cols, :] = rows.T.astype(BF16)
        f3 = feat3[...]
        f5 = feat5[...]
        p = pieces(f3, BF16, 3)
        x3[:, cols] = jnp.concatenate(p + [jnp.zeros_like(f3)], 0).astype(BF16)
        p = pieces(f5, BF16, 3)
        x5[:, cols] = jnp.concatenate(p + [jnp.zeros_like(f3)], 0).astype(BF16)
        return 0

    lax.fori_loop(0, slots, fill, 0)

    pos = [home_ref[k : k + 1, :] for k in range(3)]
    for k in range(3):
        dist8[k : k + 1, :] = -2.0 * pos[k]
    dist8[3:4, :] = jnp.ones_like(pos[0])
    dist8[4:5, :] = (pos[0] * pos[0] + pos[1] * pos[1] + pos[2] * pos[2]) + SMOOTH_SQ
    q = pieces(dist8[...], BF16, 3)
    rows = jnp.concatenate([q[0], q[1], q[0], q[1], q[2], q[0]], 0)
    ft[...] = rows.astype(BF16)
    o3[...] = jnp.zeros_like(o3)
    o5[...] = jnp.zeros_like(o5)

    def weigh(new, tile, chunk, part, rows_at):
        cols = pl.ds(pl.multiple_of(tile * TILE + part * LANES, LANES), LANES)
        rows = pl.ds(pl.multiple_of(chunk * CHUNK + rows_at, PIECE), PIECE)
        inverse = lax.rsqrt(dot(fs[rows, 0:K_DIST], ft[:, cols]))
        square = inverse * inverse
        cube = square * inverse
        fifth = cube * square
        at = (slice(rows_at, rows_at + PIECE), slice(part * LANES, (part + 1) * LANES))
        head = cube.astype(BF16)
        new[0][at] = head
        new[1][at] = (cube - head.astype(F32)).astype(BF16)
        head = fifth.astype(BF16)
        new[2][at] = head
        new[3][at] = (fifth - head.astype(F32)).astype(BF16)

    def gather(old, tile, chunk, part, which):
        cols = pl.ds(pl.multiple_of(tile * TILE + part * LANES, LANES), LANES)
        rows = pl.ds(pl.multiple_of(chunk * CHUNK, CHUNK), CHUNK)
        at = slice(part * LANES, (part + 1) * LANES)
        if which == 0:
            o3[:, cols] += dot(x3[:, rows], old[0][:, at])
        elif which == 1:
            o5[:, cols] += dot(x5[:, rows], old[2][:, at])
        elif which == 2:
            o3[0:16, cols] += dot(x3[0:16, rows], old[1][:, at])
        else:
            o5[0:48, cols] += dot(x5[0:48, rows], old[3][:, at])

    def step(index, new, old):
        following = jnp.minimum(index + 1, tiles * chunks - 1)
        new_tile, new_chunk = following // chunks, following % chunks
        tile, chunk = index // chunks, index % chunks
        each = CHUNK // PIECE // 4
        for part in range(TILE // LANES):
            for which in range(4):
                for number in range(each):
                    weigh(new, new_tile, new_chunk, part, (which * each + number) * PIECE)
                gather(old, tile, chunk, part, which)

    for part in range(TILE // LANES):
        for number in range(CHUNK // PIECE):
            weigh(first, 0, 0, part, number * PIECE)

    def two_steps(pair, _):
        step(2 * pair, second, first)
        step(2 * pair + 1, first, second)
        return 0

    lax.fori_loop(0, tiles * chunks // 2, two_steps, 0)

    sum3 = o3[0:8, :] + o3[8:16, :] + o3[16:24, :]
    sum5 = o5[0:24, :] + o5[24:48, :] + o5[48:72, :]
    factor = -INV_FOUR_PI * scale
    own = [home_ref[3 + k : 4 + k, :] for k in range(3)]
    spin = rows_of(sum3[0:3])
    turn = cross_rows(pos, spin)
    plain5 = rows_of(sum5[0:3])
    moment5 = rows_of(sum5[3:6])
    along = own[0] * pos[0] + own[1] * pos[1] + own[2] * pos[2]
    swirl, lever = [], []
    for l in range(3):
        total = along * plain5[l]
        other = along * moment5[l]
        for k in range(3):
            total -= own[k] * sum5[6 + 3 * k + l : 7 + 3 * k + l, :]
            other -= own[k] * sum5[15 + 3 * k + l : 16 + 3 * k + l, :]
        swirl.append(total)
        lever.append(other)
    twist = cross_rows(pos, swirl)
    tilt = cross_rows(own, spin)
    size = 0.0
    for k in range(3):
        row = factor * (turn[k] - sum3[3 + k : 4 + k, :])
        out_ref[k : k + 1, :] = row + carry_ref[k : k + 1, :]
        row = factor * (tilt[k] - 3.0 * (twist[k] - lever[k])) + carry_ref[3 + k : 4 + k, :]
        out_ref[3 + k : 4 + k, :] = row
        size += row * row
    peak_ref[...] = jnp.full(peak_ref.shape, jnp.max(size), F32)


def pair_sums(picks, sources, home, carry):
    slots, count = picks.shape[0], home.shape[1]
    total = slots * count
    buffers = [pltpu.VMEM((CHUNK, TILE), BF16)] * 8
    vmem = pl.BlockSpec(memory_space=pltpu.VMEM)
    return pl.pallas_call(
        functools.partial(pair_kernel, slots),
        out_shape=(
            jax.ShapeDtypeStruct((6, count), F32),
            jax.ShapeDtypeStruct((8, 128), F32),
        ),
        in_specs=[pl.BlockSpec(memory_space=pltpu.SMEM), vmem, vmem, vmem],
        out_specs=(vmem, vmem),
        scratch_shapes=[
            pltpu.VMEM((8, count), F32),
            pltpu.VMEM((24, count), F32),
            pltpu.VMEM((8, count), F32),
            pltpu.VMEM((total, 128), BF16),
            pltpu.VMEM((K_DIST, count), BF16),
            pltpu.VMEM((ROWS3, total), BF16),
            pltpu.VMEM((ROWS5, total), BF16),
            pltpu.VMEM((ROWS3, count), F32),
            pltpu.VMEM((ROWS5, count), F32),
        ]
        + buffers,
        compiler_params=pltpu.CompilerParams(vmem_limit_bytes=56 << 20),
    )(picks, sources, home, carry)


def flip(array, mask, devices):
    return lax.ppermute(array, AXES, [(i, i ^ mask) for i in range(devices)])


def visitors(home, devices):
    levels = devices.bit_length() - 1
    near = [flip(home, 1 << bit, devices) for bit in range(levels)]
    order = [bit for bit in (0, 1, 2, 4, 3, 5, 6) if bit < levels]
    order += [bit for bit in range(levels) if bit not in order]
    got, masks = [], []
    for place, last in enumerate(order[:-1]):
        others = order[place + 1 :]
        got.append(flip(jnp.stack([near[bit] for bit in others]), 1 << last, devices))
        masks += [1 << last | 1 << bit for bit in others]
    return jnp.concatenate(got, 0), masks


def body(positions, strengths, plan):
    devices = lax.axis_size(AXES)
    home = jnp.concatenate([positions, strengths], 0)
    blocks, masks = visitors(home, devices)
    own_masks = jnp.bitwise_xor(plan[:, 0], lax.axis_index(AXES).astype(jnp.int32))
    hits = own_masks[:, None] == jnp.asarray(masks, jnp.int32)[None, :]
    picks = jnp.sum(jnp.where(hits, jnp.arange(len(masks), dtype=jnp.int32)[None, :], 0), 1)
    nothing = jnp.zeros_like(home)
    partial, _ = pair_sums(jnp.zeros((1,), jnp.int32), home[None], home, nothing)
    totals, peaks = pair_sums(picks.astype(jnp.int32), blocks, home, partial)
    peak_sq = lax.pmax(peaks[0, 0], AXES)
    stretch = totals[3:]
    new_strengths = strengths + STEP_RATE / (jnp.sqrt(peak_sq) + 1e-06) * stretch
    return (totals[:3], new_strengths)


def solution(mesh):
    placed = (P(None, AXES), P(None, AXES), P(None, AXES))
    return jax.shard_map(
        body,
        mesh=mesh,
        in_specs=placed,
        out_specs=(P(None, AXES), P(None, AXES)),
        check_vma=False,
    )
```

```python
import functools
import math

import jax
import jax.numpy as jnp
from jax import lax
from jax.experimental import pallas as pl
from jax.experimental.pallas import tpu as pltpu
from jax.sharding import PartitionSpec as P

SMOOTH_SQ = 0.01
INV_FOUR_PI = 1.0 / (4.0 * math.pi)
STEP_RATE = 0.25
AXES = ("grp", "dev")
TILE = 256
PIECE = 64
LANES = 256
K_DIST = 48
ROWS3 = 16
ROWS5 = 80
BF16 = jnp.bfloat16
F32 = jnp.float32


def dot(left, right):
    return jnp.dot(left, right, preferred_element_type=F32)


def pieces(value, dtype, count):
    out = []
    for _ in range(count):
        head = value.astype(dtype).astype(F32)
        out.append(head)
        value = value - head
    return out


def cross_rows(first, second):
    return [
        first[1] * second[2] - first[2] * second[1],
        first[2] * second[0] - first[0] * second[2],
        first[0] * second[1] - first[1] * second[0],
    ]


def rows_of(block):
    return [block[k : k + 1, :] for k in range(block.shape[0])]


def pair_kernel(
    slots, chunk_size, pick_ref, src_ref, home_ref, carry_ref, out_ref, peak_ref,
    feat3, feat5, dist8, fs, ft, x3, x5, o3, o5, *bufs
):
    count = home_ref.shape[1]
    width = src_ref.shape[2]
    chunks = slots * width // chunk_size
    tiles = count // TILE
    first, second = bufs[:4], bufs[4:]

    largest = jnp.max(jnp.abs(src_ref[pick_ref[0], 3:6, :]))
    for slot in range(1, slots):
        largest = jnp.maximum(largest, jnp.max(jnp.abs(src_ref[pick_ref[slot], 3:6, :])))
    scale = jnp.maximum(largest, 1e-30)

    feat3[...] = jnp.zeros_like(feat3)
    dist8[...] = jnp.zeros_like(dist8)

    def fill(slot, _):
        block = src_ref[pick_ref[slot]]
        cols = pl.ds(pl.multiple_of(slot * width, width), width)
        pos = rows_of(block[0:3])
        strength = rows_of(block[3:6] / scale)
        moment = cross_rows(pos, strength)
        for k in range(3):
            feat3[k : k + 1, :] = strength[k]
            feat3[3 + k : 4 + k, :] = moment[k]
            feat5[k : k + 1, :] = strength[k]
            feat5[3 + k : 4 + k, :] = moment[k]
            for l in range(3):
                feat5[6 + 3 * k + l : 7 + 3 * k + l, :] = pos[k] * strength[l]
                feat5[15 + 3 * k + l : 16 + 3 * k + l, :] = pos[k] * moment[l]
            dist8[k : k + 1, 0:width] = pos[k]
        dist8[3:4, 0:width] = pos[0] * pos[0] + pos[1] * pos[1] + pos[2] * pos[2]
        dist8[4:5, 0:width] = jnp.ones_like(pos[0])
        q = pieces(dist8[:, 0:width], BF16, 3)
        rows = jnp.concatenate([q[0], q[0], q[1], q[1], q[0], q[2]], 0)
        rows = jnp.concatenate([rows, jnp.zeros((128 - K_DIST, width), F32)], 0)
        fs[cols, :] = rows.T.astype(BF16)
        f3 = feat3[...]
        f5 = feat5[...]
        x3[:, cols] = jnp.concatenate(pieces(f3, BF16, 2), 0).astype(BF16)
        p = pieces(f5, BF16, 3)
        x5[:, cols] = jnp.concatenate(p + [jnp.zeros_like(f3)], 0).astype(BF16)
        return 0

    lax.fori_loop(0, slots, fill, 0)

    pos = [home_ref[k : k + 1, :] for k in range(3)]
    for k in range(3):
        dist8[k : k + 1, :] = -2.0 * pos[k]
    dist8[3:4, :] = jnp.ones_like(pos[0])
    dist8[4:5, :] = (pos[0] * pos[0] + pos[1] * pos[1] + pos[2] * pos[2]) + SMOOTH_SQ
    q = pieces(dist8[...], BF16, 3)
    rows = jnp.concatenate([q[0], q[1], q[0], q[1], q[2], q[0]], 0)
    ft[...] = rows.astype(BF16)
    o3[...] = jnp.zeros_like(o3)
    o5[...] = jnp.zeros_like(o5)

    def weigh(new, tile, chunk, part, rows_at):
        cols = pl.ds(pl.multiple_of(tile * TILE + part * LANES, LANES), LANES)
        rows = pl.ds(pl.multiple_of(chunk * chunk_size + rows_at, PIECE), PIECE)
        inverse = lax.rsqrt(dot(fs[rows, 0:K_DIST], ft[:, cols]))
        square = inverse * inverse
        cube = square * inverse
        fifth = cube * square
        at = (slice(rows_at, rows_at + PIECE), slice(part * LANES, (part + 1) * LANES))
        head = cube.astype(BF16)
        new[0][at] = head
        new[1][at] = (cube - head.astype(F32)).astype(BF16)
        head = fifth.astype(BF16)
        new[2][at] = head
        new[3][at] = (fifth - head.astype(F32)).astype(BF16)

    def gather(old, tile, chunk, part, which):
        cols = pl.ds(pl.multiple_of(tile * TILE + part * LANES, LANES), LANES)
        rows = pl.ds(pl.multiple_of(chunk * chunk_size, chunk_size), chunk_size)
        at = slice(part * LANES, (part + 1) * LANES)
        if which == 0:
            o3[:, cols] += dot(x3[:, rows], old[0][:, at])
        elif which == 1:
            o5[:, cols] += dot(x5[:, rows], old[2][:, at])
        elif which == 2:
            o3[0:16, cols] += dot(x3[0:16, rows], old[1][:, at])
        else:
            o5[0:48, cols] += dot(x5[0:48, rows], old[3][:, at])

    def step(index, new, old):
        following = jnp.minimum(index + 1, tiles * chunks - 1)
        new_tile, new_chunk = following // chunks, following % chunks
        tile, chunk = index // chunks, index % chunks
        each = chunk_size // PIECE // 4
        for part in range(TILE // LANES):
            for which in range(4):
                for number in range(each):
                    weigh(new, new_tile, new_chunk, part, (which * each + number) * PIECE)
                gather(old, tile, chunk, part, which)

    for part in range(TILE // LANES):
        for number in range(chunk_size // PIECE):
            weigh(first, 0, 0, part, number * PIECE)

    def two_steps(pair, _):
        step(2 * pair, second, first)
        step(2 * pair + 1, first, second)
        return 0

    lax.fori_loop(0, tiles * chunks // 2, two_steps, 0)

    sum3 = o3[0:8, :] + o3[8:16, :]
    sum5 = o5[0:24, :] + o5[24:48, :] + o5[48:72, :]
    factor = -INV_FOUR_PI * scale
    own = [home_ref[3 + k : 4 + k, :] for k in range(3)]
    spin = rows_of(sum3[0:3])
    turn = cross_rows(pos, spin)
    plain5 = rows_of(sum5[0:3])
    moment5 = rows_of(sum5[3:6])
    along = own[0] * pos[0] + own[1] * pos[1] + own[2] * pos[2]
    swirl, lever = [], []
    for l in range(3):
        total = along * plain5[l]
        other = along * moment5[l]
        for k in range(3):
            total -= own[k] * sum5[6 + 3 * k + l : 7 + 3 * k + l, :]
            other -= own[k] * sum5[15 + 3 * k + l : 16 + 3 * k + l, :]
        swirl.append(total)
        lever.append(other)
    twist = cross_rows(pos, swirl)
    tilt = cross_rows(own, spin)
    size = 0.0
    for k in range(3):
        row = factor * (turn[k] - sum3[3 + k : 4 + k, :])
        out_ref[k : k + 1, :] = row + carry_ref[k : k + 1, :]
        row = factor * (tilt[k] - 3.0 * (twist[k] - lever[k])) + carry_ref[3 + k : 4 + k, :]
        out_ref[3 + k : 4 + k, :] = row
        size += row * row
    peak_ref[...] = jnp.full(peak_ref.shape, jnp.max(size), F32)


def pair_sums(picks, sources, home, carry, chunk_size=1024):
    slots, width, count = picks.shape[0], sources.shape[2], home.shape[1]
    total = slots * width
    buffers = [pltpu.VMEM((chunk_size, TILE), BF16)] * 8
    vmem = pl.BlockSpec(memory_space=pltpu.VMEM)
    return pl.pallas_call(
        functools.partial(pair_kernel, slots, chunk_size),
        out_shape=(
            jax.ShapeDtypeStruct((6, count), F32),
            jax.ShapeDtypeStruct((128, 128), F32),
        ),
        in_specs=[pl.BlockSpec(memory_space=pltpu.SMEM), vmem, vmem, vmem],
        out_specs=(vmem, vmem),
        scratch_shapes=[
            pltpu.VMEM((8, width), F32),
            pltpu.VMEM((24, width), F32),
            pltpu.VMEM((8, count), F32),
            pltpu.VMEM((total, 128), BF16),
            pltpu.VMEM((K_DIST, count), BF16),
            pltpu.VMEM((ROWS3, total), BF16),
            pltpu.VMEM((ROWS5, total), BF16),
            pltpu.VMEM((ROWS3, count), F32),
            pltpu.VMEM((ROWS5, count), F32),
        ]
        + buffers,
        compiler_params=pltpu.CompilerParams(vmem_limit_bytes=56 << 20),
    )(picks, sources, home, carry)


def flip(array, mask, devices):
    return lax.ppermute(array, AXES, [(i, i ^ mask) for i in range(devices)])


def near_blocks(home, devices):
    levels = devices.bit_length() - 1
    return [flip(home, 1 << bit, devices) for bit in range(levels)]


def far_stacks(near):
    levels = len(near)
    order = [bit for bit in (0, 1, 2, 4, 3, 5, 6) if bit < levels]
    order += [bit for bit in range(levels) if bit not in order]
    stacks, lasts, masks = [], [], []
    for place, last in enumerate(order[:-1]):
        others = order[place + 1 :]
        stacks.append(jnp.stack([near[bit] for bit in others]))
        lasts.append(1 << last)
        masks += [1 << last | 1 << bit for bit in others]
    return stacks, lasts, masks


def body(positions, strengths, plan):
    devices = lax.axis_size(AXES)
    home = jnp.concatenate([positions, strengths], 0)
    half = home.shape[1] // 2
    near = near_blocks(home, devices)
    zero = jnp.zeros((1,), jnp.int32)
    partial, _ = pair_sums(zero, home[None, :, :half], home, jnp.zeros_like(home), 512)
    stacks, lasts, masks = far_stacks(near)
    own_masks = jnp.bitwise_xor(plan[:, 0], lax.axis_index(AXES).astype(jnp.int32))
    hits = own_masks[:, None] == jnp.asarray(masks, jnp.int32)[None, :]
    picks = jnp.sum(jnp.where(hits, jnp.arange(len(masks), dtype=jnp.int32)[None, :], 0), 1)
    partial, stacks = lax.optimization_barrier((partial, stacks))
    far = [flip(stack, last, devices) for stack, last in zip(stacks, lasts)]
    partial, _ = pair_sums(zero, home[None, :, half:], home, partial, 512)
    totals, peaks = pair_sums(picks.astype(jnp.int32), jnp.concatenate(far, 0), home, partial)
    every = lax.all_to_all(peaks[0:devices], AXES, 0, 0, tiled=True)
    peak_sq = jnp.max(every)
    stretch = totals[3:]
    new_strengths = strengths + STEP_RATE / (jnp.sqrt(peak_sq) + 1e-06) * stretch
    return (totals[:3], new_strengths)


def solution(mesh):
    placed = (P(None, AXES), P(None, AXES), P(None, AXES))
    return jax.shard_map(
        body,
        mesh=mesh,
        in_specs=placed,
        out_specs=(P(None, AXES), P(None, AXES)),
        check_vma=False,
    )
```

```python
import functools
import math

import jax
import jax.numpy as jnp
from jax import lax
from jax.experimental import pallas as pl
from jax.experimental.pallas import tpu as pltpu
from jax.sharding import PartitionSpec as P

SMOOTH_SQ = 0.01
INV_FOUR_PI = 1.0 / (4.0 * math.pi)
STEP_RATE = 0.25
AXES = ("grp", "dev")
TILE = 256
PIECE = 64
LANES = 256
K_DIST = 48
ROWS3 = 32
ROWS5 = 64
BF16 = jnp.bfloat16
F32 = jnp.float32


def dot(left, right):
    return jnp.dot(left, right, preferred_element_type=F32)


def pieces(value, dtype, count):
    out = []
    for _ in range(count):
        head = value.astype(dtype).astype(F32)
        out.append(head)
        value = value - head
    return out


def cross_rows(first, second):
    return [
        first[1] * second[2] - first[2] * second[1],
        first[2] * second[0] - first[0] * second[2],
        first[0] * second[1] - first[1] * second[0],
    ]


def rows_of(block):
    return [block[k : k + 1, :] for k in range(block.shape[0])]


def pair_kernel(
    slots, chunk_size, pick_ref, src_ref, home_ref, carry_ref, out_ref, peak_ref,
    feat3, feat5, stack5, dist8, fs, ft, x3, x5, o3, o5, *bufs
):
    count = home_ref.shape[1]
    width = src_ref.shape[2]
    chunks = slots * width // chunk_size
    tiles = count // TILE
    first, second = bufs[:4], bufs[4:]

    largest = jnp.max(jnp.abs(src_ref[pick_ref[0], 3:6, :]))
    for slot in range(1, slots):
        largest = jnp.maximum(largest, jnp.max(jnp.abs(src_ref[pick_ref[slot], 3:6, :])))
    scale = jnp.maximum(largest, 1e-30)

    feat3[...] = jnp.zeros_like(feat3)
    stack5[...] = jnp.zeros_like(stack5)
    dist8[...] = jnp.zeros_like(dist8)

    def fill(slot, _):
        block = src_ref[pick_ref[slot]]
        cols = pl.ds(pl.multiple_of(slot * width, width), width)
        pos = rows_of(block[0:3])
        strength = rows_of(block[3:6] / scale)
        moment = cross_rows(pos, strength)
        for k in range(3):
            feat3[k : k + 1, :] = strength[k]
            feat3[3 + k : 4 + k, :] = moment[k]
            feat5[k : k + 1, :] = strength[k]
            feat5[3 + k : 4 + k, :] = moment[k]
            feat5[6 + k : 7 + k, :] = pos[k] * strength[k]
            feat5[9 + k : 10 + k, :] = pos[k] * strength[(k + 1) % 3]
            for l in range(3 if k < 2 else 2):
                feat5[12 + 3 * k + l : 13 + 3 * k + l, :] = pos[k] * moment[l]
            dist8[k : k + 1, 0:width] = pos[k]
        dist8[3:4, 0:width] = pos[0] * pos[0] + pos[1] * pos[1] + pos[2] * pos[2]
        dist8[4:5, 0:width] = jnp.ones_like(pos[0])
        q = pieces(dist8[:, 0:width], BF16, 3)
        rows = jnp.concatenate([q[0], q[0], q[1], q[1], q[0], q[2]], 0)
        rows = jnp.concatenate([rows, jnp.zeros((128 - K_DIST, width), F32)], 0)
        fs[cols, :] = rows.T.astype(BF16)
        f3 = feat3[...]
        f5 = feat5[...]
        p = pieces(f3, BF16, 3)
        x3[:, cols] = jnp.concatenate(p + [jnp.zeros_like(f3)], 0).astype(BF16)
        for number, part in enumerate(pieces(f5, BF16, 3)):
            stack5[20 * number : 20 * number + 20, :] = part
        x5[:, cols] = stack5[...].astype(BF16)
        return 0

    lax.fori_loop(0, slots, fill, 0)

    pos = [home_ref[k : k + 1, :] for k in range(3)]
    for k in range(3):
        dist8[k : k + 1, :] = -2.0 * pos[k]
    dist8[3:4, :] = jnp.ones_like(pos[0])
    dist8[4:5, :] = (pos[0] * pos[0] + pos[1] * pos[1] + pos[2] * pos[2]) + SMOOTH_SQ
    q = pieces(dist8[...], BF16, 3)
    rows = jnp.concatenate([q[0], q[1], q[0], q[1], q[2], q[0]], 0)
    ft[...] = rows.astype(BF16)
    o3[...] = jnp.zeros_like(o3)
    o5[...] = jnp.zeros_like(o5)

    def weigh(new, tile, chunk, part, rows_at):
        cols = pl.ds(pl.multiple_of(tile * TILE + part * LANES, LANES), LANES)
        rows = pl.ds(pl.multiple_of(chunk * chunk_size + rows_at, PIECE), PIECE)
        inverse = lax.rsqrt(dot(fs[rows, 0:K_DIST], ft[:, cols]))
        square = inverse * inverse
        cube = square * inverse
        fifth = cube * square
        at = (slice(rows_at, rows_at + PIECE), slice(part * LANES, (part + 1) * LANES))
        head = cube.astype(BF16)
        new[0][at] = head
        new[1][at] = (cube - head.astype(F32)).astype(BF16)
        head = fifth.astype(BF16)
        new[2][at] = head
        new[3][at] = (fifth - head.astype(F32)).astype(BF16)

    def gather(old, tile, chunk, part, which):
        cols = pl.ds(pl.multiple_of(tile * TILE + part * LANES, LANES), LANES)
        rows = pl.ds(pl.multiple_of(chunk * chunk_size, chunk_size), chunk_size)
        at = slice(part * LANES, (part + 1) * LANES)
        if which == 0:
            o3[:, cols] += dot(x3[:, rows], old[0][:, at])
        elif which == 1:
            o5[:, cols] += dot(x5[:, rows], old[2][:, at])
        elif which == 2:
            o3[0:16, cols] += dot(x3[0:16, rows], old[1][:, at])
        else:
            o5[0:48, cols] += dot(x5[0:48, rows], old[3][:, at])

    def step(index, new, old):
        following = jnp.minimum(index + 1, tiles * chunks - 1)
        new_tile, new_chunk = following // chunks, following % chunks
        tile, chunk = index // chunks, index % chunks
        each = chunk_size // PIECE // 4
        for part in range(TILE // LANES):
            for which in range(4):
                for number in range(each):
                    weigh(new, new_tile, new_chunk, part, (which * each + number) * PIECE)
                gather(old, tile, chunk, part, which)

    for part in range(TILE // LANES):
        for number in range(chunk_size // PIECE):
            weigh(first, 0, 0, part, number * PIECE)

    def two_steps(pair, _):
        step(2 * pair, second, first)
        step(2 * pair + 1, first, second)
        return 0

    lax.fori_loop(0, tiles * chunks // 2, two_steps, 0)

    sum3 = o3[0:8, :] + o3[8:16, :] + o3[16:24, :]
    sum5 = o5[0:20, :] + o5[20:40, :] + o5[40:60, :]
    factor = -INV_FOUR_PI * scale
    own = [home_ref[3 + k : 4 + k, :] for k in range(3)]
    spin = rows_of(sum3[0:3])
    turn = cross_rows(pos, spin)
    plain5 = rows_of(sum5[0:3])
    moment5 = rows_of(sum5[3:6])
    along = own[0] * pos[0] + own[1] * pos[1] + own[2] * pos[2]
    swirl, lever = [], []
    cross = [[None] * 3 for _ in range(3)]
    arm = [[None] * 3 for _ in range(3)]
    for k in range(3):
        after = (k + 1) % 3
        cross[k][k] = sum5[6 + k : 7 + k, :]
        cross[k][after] = sum5[9 + k : 10 + k, :]
        cross[after][k] = cross[k][after] - moment5[(k + 2) % 3]
        for l in range(3 if k < 2 else 2):
            arm[k][l] = sum5[12 + 3 * k + l : 13 + 3 * k + l, :]
    arm[2][2] = -(arm[0][0] + arm[1][1])
    for l in range(3):
        total = along * plain5[l]
        other = along * moment5[l]
        for k in range(3):
            total -= own[k] * cross[k][l]
            other -= own[k] * arm[k][l]
        swirl.append(total)
        lever.append(other)
    twist = cross_rows(pos, swirl)
    tilt = cross_rows(own, spin)
    size = 0.0
    for k in range(3):
        row = factor * (turn[k] - sum3[3 + k : 4 + k, :])
        out_ref[k : k + 1, :] = row + carry_ref[k : k + 1, :]
        row = factor * (tilt[k] - 3.0 * (twist[k] - lever[k])) + carry_ref[3 + k : 4 + k, :]
        out_ref[3 + k : 4 + k, :] = row
        size += row * row
    peak_ref[...] = jnp.full(peak_ref.shape, jnp.max(size), F32)


def pair_sums(picks, sources, home, carry, chunk_size=1024):
    slots, width, count = picks.shape[0], sources.shape[2], home.shape[1]
    total = slots * width
    buffers = [pltpu.VMEM((chunk_size, TILE), BF16)] * 8
    vmem = pl.BlockSpec(memory_space=pltpu.VMEM)
    return pl.pallas_call(
        functools.partial(pair_kernel, slots, chunk_size),
        out_shape=(
            jax.ShapeDtypeStruct((6, count), F32),
            jax.ShapeDtypeStruct((128, 128), F32),
        ),
        in_specs=[pl.BlockSpec(memory_space=pltpu.SMEM), vmem, vmem, vmem],
        out_specs=(vmem, vmem),
        scratch_shapes=[
            pltpu.VMEM((8, width), F32),
            pltpu.VMEM((20, width), F32),
            pltpu.VMEM((ROWS5, width), F32),
            pltpu.VMEM((8, count), F32),
            pltpu.VMEM((total, 128), BF16),
            pltpu.VMEM((K_DIST, count), BF16),
            pltpu.VMEM((ROWS3, total), BF16),
            pltpu.VMEM((ROWS5, total), BF16),
            pltpu.VMEM((ROWS3, count), F32),
            pltpu.VMEM((ROWS5, count), F32),
        ]
        + buffers,
        compiler_params=pltpu.CompilerParams(vmem_limit_bytes=56 << 20),
    )(picks, sources, home, carry)


def flip(array, mask, devices):
    return lax.ppermute(array, AXES, [(i, i ^ mask) for i in range(devices)])


def near_blocks(home, devices):
    levels = devices.bit_length() - 1
    return [flip(home, 1 << bit, devices) for bit in range(levels)]


def far_stacks(near):
    levels = len(near)
    order = [bit for bit in (0, 1, 2, 4, 3, 5, 6) if bit < levels]
    order += [bit for bit in range(levels) if bit not in order]
    stacks, lasts, masks = [], [], []
    for place, last in enumerate(order[:-1]):
        others = order[place + 1 :]
        stacks.append(jnp.stack([near[bit] for bit in others]))
        lasts.append(1 << last)
        masks += [1 << last | 1 << bit for bit in others]
    return stacks, lasts, masks


def body(positions, strengths, plan):
    devices = lax.axis_size(AXES)
    home = jnp.concatenate([positions, strengths], 0)
    third = home.shape[1] // 3
    near = near_blocks(home, devices)
    zero = jnp.zeros((1,), jnp.int32)
    partial, _ = pair_sums(zero, home[None, :, :third], home, jnp.zeros_like(home), 512)
    stacks, lasts, masks = far_stacks(near)
    own_masks = jnp.bitwise_xor(plan[:, 0], lax.axis_index(AXES).astype(jnp.int32))
    hits = own_masks[:, None] == jnp.asarray(masks, jnp.int32)[None, :]
    picks = jnp.sum(jnp.where(hits, jnp.arange(len(masks), dtype=jnp.int32)[None, :], 0), 1)
    partial, stacks = lax.optimization_barrier((partial, stacks))
    far = [flip(stack, last, devices) for stack, last in zip(stacks, lasts)]
    partial, _ = pair_sums(zero, home[None, :, third:], home, partial, 512)
    totals, peaks = pair_sums(picks.astype(jnp.int32), jnp.concatenate(far, 0), home, partial)
    every = lax.all_to_all(peaks[0:devices], AXES, 0, 0, tiled=True)
    peak_sq = jnp.max(every)
    stretch = totals[3:]
    new_strengths = strengths + STEP_RATE / (jnp.sqrt(peak_sq) + 1e-06) * stretch
    return (totals[:3], new_strengths)


def solution(mesh):
    placed = (P(None, AXES), P(None, AXES), P(None, AXES))
    return jax.shard_map(
        body,
        mesh=mesh,
        in_specs=placed,
        out_specs=(P(None, AXES), P(None, AXES)),
        check_vma=False,
    )
```
